512 devices in a mesh: ka: 64 (over z_lo, y, core), ga: 8 (over z_hi, x).
Axes of the slice: x: 4, y: 8, z: 8 (z_hi: 2, z_lo: 4; z = z_hi * 4 + z_lo), core: 2. Of those that a mesh axis runs over, the one named last changes fastest.
Arguments:
- coeffs: bfloat16 [3584, 2, 30720], P('ka', None, 'ga'), may hold values from -1 to 1
- shift_maps: int32 [8, 3, 30720], P(None, None, 'ga'), may hold values from 0 to 30719, as said below
Outputs:
- intersections: float32 [448, 3, 2, 3584], P('ga', None, None, 'ka')
The draws below stay inside these ranges and needn't reach their ends.
Inputs may be any that keep to these rules, and one draw needn't show every extreme that they name: `shift_maps`: for every k-point and b-vector the row is a permutation of the plane waves that maps each aligned block of 128 plane waves onto itself.
All inputs are finite; a program needn't handle non-finite values.
Results may differ from the reference program's by a relative error of at most 0.0003.
Values may be sent and summed in bfloat16 or wider, within the bound.
No kernel may reach another device: no remote copies, remote signals or barrier semaphores. Data moves between devices by JAX's collectives and lax.ppermute only.
A program may use at most 64 MiB of HBM per device.

```python
import jax
import jax.numpy as jnp
from jax import lax

NB = 448
NPW = 30720
KPTS = 8


def draw_shift_maps(key, part):
    key = jax.random.fold_in(key, 7)
    blocks = NPW // 128
    keys = jax.random.split(key, KPTS * 3 * blocks)
    inside = jax.vmap(lambda single: jax.random.permutation(single, 128))(keys)
    inside = inside.reshape(KPTS, 3, blocks, 128).astype(jnp.int32)
    starts = (jnp.arange(blocks, dtype=jnp.int32) * 128)[:, None]
    return (inside + starts).reshape(KPTS, 3, NPW).astype(jnp.int32)


def steps_of(rng, dims, cuts, low, top_value):
    def one(position, blocks):
        heights = jax.random.uniform(jax.random.fold_in(jax.random.fold_in(rng, 6), position), (blocks,), jnp.float32, low / len(cuts), top_value / len(cuts))
        return jnp.repeat(jnp.exp(heights), dims[position] // blocks).reshape((-1,) + (1,) * (len(dims) - position - 1))

    factor_of = one(*cuts[0])
    for cut in cuts[1:]:
        factor_of = factor_of * one(*cut)
    return factor_of


def centred(key, shape, scale, most, shards=(), kind=jnp.bfloat16):
    result = scale * jax.random.normal(key, shape, jnp.float32)
    if shards:
        result = result * steps_of(key, shape, shards, -0.22, 0.18)
    return jnp.clip(result, -most, most).astype(kind)


def setup_inputs(seed: int = 0) -> dict:
    key_of = jax.random.split(jax.random.key(seed), 3)
    return {
        "coeffs": centred(key_of[0], (KPTS * NB, 2, NPW), 0.065, 1.0, ((0, 64), (2, 8))),
        "shift_maps": draw_shift_maps(jax.random.fold_in(key_of[2], 71), 0),
    }


def reference(coeffs, shift_maps):
    blocks = coeffs.reshape(KPTS, NB, 2, NPW)
    columns = []
    for kpoint in range(KPTS):
        moved = [jnp.take(blocks[kpoint ^ (1 << bvec)], shift_maps[kpoint, bvec].astype(jnp.int32), axis=2) for bvec in range(3)]
        right = jnp.concatenate(moved, axis=0).reshape(3 * NB * 2, NPW)
        left = blocks[kpoint].reshape(NB * 2, NPW)
        product = lax.dot_general(left, right, (((1,), (1,)), ((), ())), preferred_element_type=jnp.float32)
        product = product.reshape(NB, 2, 3, NB, 2)
        real_part = product[:, 0, :, :, 0] + product[:, 1, :, :, 1]
        imag_part = product[:, 0, :, :, 1] - product[:, 1, :, :, 0]
        columns.append(jnp.stack([real_part, imag_part], axis=2))
    return jnp.concatenate(columns, axis=3)
```

```python
import functools

import jax
import jax.numpy as jnp
from jax import lax
from jax.experimental import pallas as pl
from jax.experimental.pallas import tpu as pltpu
from jax.sharding import PartitionSpec as P

CORES = 2
YS = 8
HALF = YS // 2
LANES = 128


def place(i):
    return i // (YS * CORES), i // CORES % YS, i % CORES


def number(z, y, c):
    return (z * YS + y % YS) * CORES + c


def moved(shard, target, wanted=None):
    pairs = [(i, number(*target(*place(i)))) for i in range(lax.axis_size("ka"))]
    if wanted is not None:
        pairs = [(s, t) for s, t in pairs if wanted(*place(t))]
    return lax.ppermute(shard, "ka", pairs)


def to_sibling(z, y, c):
    return z, y, 1 - c


def along_y(z, y, c):
    return z, y + 1 - 2 * c, c


def wanted_from_sibling(hops):
    def wanted(z, y, c):
        return hops <= (HALF - 1 - y % HALF if c == 0 else y % HALF)

    return wanted


def after(shard, *others):
    return lax.optimization_barrier((shard, *others))[0]


def products_kernel(nb, has_rest, *refs):
    refs = list(refs)
    where, maps, own, sibling = refs[:4]
    del refs[:4]
    ga, gb, sa, sb = (refs[3 * i : 3 * i + 3] for i in range(4))
    del refs[:12]
    rights = refs[:nb]
    del refs[:nb]
    rest = refs.pop(0) if has_rest else None
    out, left, raw, right, total, left_sems, raw_sems = refs
    rows, width = own.shape
    half = rows // 2
    yy, core = where[0], where[1]
    reach = jnp.where(core == 0, yy, HALF - 1 - yy)

    def slot(s):
        return left.at[pl.ds(s * rows, rows)]

    for b in range(nb):
        pltpu.make_async_copy(rights[b], raw.at[b], raw_sems.at[b]).start()
    pltpu.make_async_copy(own, slot(0), left_sems.at[0]).start()
    pltpu.make_async_copy(sibling, slot(1), left_sems.at[1]).start()
    for d in range(1, HALF):
        for part, (near, far) in enumerate(((ga, sb), (gb, sa))):
            s = 2 * d + part

            @pl.when(d <= reach)
            def _():
                pltpu.make_async_copy(near[d - 1], slot(s), left_sems.at[s]).start()

            @pl.when(d > reach)
            def _():
                pltpu.make_async_copy(far[HALF - d - 1], slot(s), left_sems.at[s]).start()

    right[...] = jnp.zeros_like(right)
    inside = lax.broadcasted_iota(jnp.int32, (LANES, LANES), 0)
    for b in range(nb):
        pltpu.make_async_copy(rights[b], raw.at[b], raw_sems.at[b]).wait()
    blocks = 5

    @pl.loop(0, width // (LANES * blocks))
    def _(j):
        for i in range(blocks):
            at = pl.ds(pl.multiple_of((j * blocks + i) * LANES, LANES), LANES)
            for b in range(nb):
                chosen = jnp.where(inside == maps[b : b + 1, at], 1.0, 0.0).astype(jnp.bfloat16)
                right[pl.ds(b * LANES, rows), at] = jnp.dot(
                    raw[b, :, at], chosen, preferred_element_type=jnp.float32
                ).astype(jnp.bfloat16)

    for s in range(8):
        pltpu.make_async_copy(own, slot(s), left_sems.at[s]).wait()
    chunk = 1280
    for j in range(width // chunk):
        at = pl.ds(j * chunk, chunk)
        part = lax.dot_general(
            left[:, at], right[:, at], (((1,), (1,)), ((), ())), preferred_element_type=jnp.float32
        )
        total[...] = part if j == 0 else total[...] + part

    first = 0
    if has_rest:
        first = 1
        out[:, pl.ds(1, 2)] = rest[...]
    for s in range(8):
        d, other = s // 2, s % 2
        chip = jnp.where(core == 0, yy + HALF - d, yy + d) % HALF
        block = chip * CORES + jnp.where(other == 0, core, 1 - core)
        for b in range(nb):
            lanes = pl.ds(b * LANES, LANES)
            top = total[pl.ds(s * rows, half), lanes]
            low = total[pl.ds(s * rows + half, half), lanes]
            turned = jnp.concatenate(
                [low[:, half:rows], -low[:, :half], jnp.zeros((half, LANES - rows), jnp.float32)], axis=1
            )
            out[block, 0 if has_rest else core ^ b] = top + turned


def products(where, maps, lefts, rights, rest=None):
    nb = len(rights)
    rows, width = lefts[0].shape
    anywhere = pl.BlockSpec(memory_space=pl.ANY)
    vmem = pl.BlockSpec(memory_space=pltpu.VMEM)
    extra = [] if rest is None else [rest]
    return pl.pallas_call(
        functools.partial(products_kernel, nb, rest is not None),
        out_shape=jax.ShapeDtypeStruct((8, nb + 2 * len(extra), rows // 2, LANES), jnp.float32),
        in_specs=[pl.BlockSpec(memory_space=pltpu.SMEM), vmem]
        + [anywhere] * (len(lefts) + nb)
        + [vmem] * len(extra),
        out_specs=vmem,
        scratch_shapes=[
            pltpu.VMEM((8 * rows, width), jnp.bfloat16),
            pltpu.VMEM((nb, rows, width), jnp.bfloat16),
            pltpu.VMEM((nb * LANES, width), jnp.bfloat16),
            pltpu.VMEM((8 * rows, nb * LANES), jnp.float32),
            pltpu.SemaphoreType.DMA((8,)),
            pltpu.SemaphoreType.DMA((nb,)),
        ],
        compiler_params=pltpu.CompilerParams(vmem_limit_bytes=40 * 2**20),
        cost_estimate=pl.CostEstimate(
            flops=2 * 8 * rows * nb * LANES * width,
            bytes_accessed=(8 + nb) * rows * width * 2,
            transcendentals=0,
        ),
    )(where, maps, *lefts, *rights, *extra)


def along_z(z, y, c):
    return z ^ (1 + c), y, c


def per_device(coeffs, shift_maps):
    bands, _, width = coeffs.shape
    position = lax.axis_index("ka")
    core = position % CORES
    yy = position // CORES % HALF
    where = jnp.stack([yy, core]).astype(jnp.int32)
    kpoint = position // (CORES * HALF)
    maps = lax.dynamic_index_in_dim(shift_maps, kpoint, 0, keepdims=False) % LANES
    later_maps = jnp.where(core == 0, maps[1:], maps[:0:-1])
    mine = coeffs.transpose(1, 0, 2).reshape(2 * bands, width)

    sibling = moved(mine, to_sibling)
    za = moved(mine, along_z)
    zb = moved(after(sibling, za), along_z)
    ga, gb, sa, sb = [mine], [sibling], [None], [None]
    for hops in range(1, HALF):
        deps = {1: [], 2: [], 3: [za, sa[1], sb[1]] if hops == 3 else []}[hops]
        ga.append(moved(after(ga[-1], *deps), along_y))
        gb.append(moved(gb[-1], along_y))
        sa.append(moved(ga[-1], to_sibling, wanted_from_sibling(hops)))
        sb.append(moved(gb[-1], to_sibling, wanted_from_sibling(hops)))
    opposite = moved(after(ga[-1], zb, sa[2], sb[2]), along_y)
    zs = moved(zb, to_sibling)
    lefts = [mine, sibling, *ga[1:], *gb[1:], *sa[1:], *sb[1:]]
    later = products(where, later_maps, lefts, [za, zs])
    every = products(where, maps[:1], lefts, [opposite], later)
    shares = lax.all_to_all(every, "ga", 0, 0, tiled=True)
    total = shares.sum(axis=0)[:, :, : 2 * bands]
    return total.transpose(1, 0, 2).reshape(bands, 3, 2, bands)


def solution(mesh):
    return jax.shard_map(
        per_device,
        mesh=mesh,
        in_specs=(P("ka", None, "ga"), P(None, None, "ga")),
        out_specs=P("ga", None, None, "ka"),
        check_vma=False,
    )
```

```python
import functools

import jax
import jax.numpy as jnp
from jax import lax
from jax.experimental import pallas as pl
from jax.experimental.pallas import tpu as pltpu
from jax.sharding import PartitionSpec as P

CORES = 2
YS = 8
HALF = YS // 2
LANES = 128


def place(i):
    return i // (YS * CORES), i // CORES % YS, i % CORES


def number(z, y, c):
    return (z * YS + y % YS) * CORES + c


def moved(shard, target, wanted=None):
    pairs = [(i, number(*target(*place(i)))) for i in range(lax.axis_size("ka"))]
    if wanted is not None:
        pairs = [(s, t) for s, t in pairs if wanted(*place(t))]
    return lax.ppermute(shard, "ka", pairs)


def to_sibling(z, y, c):
    return z, y, 1 - c


def along_y(z, y, c):
    return z, y + 1 - 2 * c, c


def wanted_from_sibling(hops):
    def wanted(z, y, c):
        return hops <= (HALF - 1 - y % HALF if c == 0 else y % HALF)

    return wanted


def after(shard, *others):
    return lax.optimization_barrier((shard, *others))[0]


def scaled(values, exponent_lane):
    most = jnp.max(jnp.abs(values), axis=1, keepdims=True)
    exponent = jnp.maximum(jnp.ceil(jnp.log2(jnp.maximum(most, 1e-30) / 32766.0)), -120.0)
    whole = jnp.round(values * jnp.exp2(-exponent))
    lane = lax.broadcasted_iota(jnp.int32, values.shape, 1)
    return jnp.where(lane == exponent_lane, exponent, whole).astype(jnp.int32).astype(jnp.int16)


def products_kernel(nb, has_rest, *refs):
    refs = list(refs)
    where, maps, own, sibling = refs[:4]
    del refs[:4]
    ga, gb, sa, sb = (refs[3 * i : 3 * i + 3] for i in range(4))
    del refs[:12]
    rights = refs[:nb]
    del refs[:nb]
    rest = refs.pop(0) if has_rest else None
    out, left, raw, right, total, left_sems, raw_sems = refs
    rows, width = own.shape
    half = rows // 2
    yy, core = where[0], where[1]
    reach = jnp.where(core == 0, yy, HALF - 1 - yy)

    def slot(s):
        return left.at[pl.ds(s * rows, rows)]

    for b in range(nb):
        pltpu.make_async_copy(rights[b], raw.at[b], raw_sems.at[b]).start()
    pltpu.make_async_copy(own, slot(0), left_sems.at[0]).start()
    pltpu.make_async_copy(sibling, slot(1), left_sems.at[1]).start()
    for d in range(1, HALF):
        for part, (near, far) in enumerate(((ga, sb), (gb, sa))):
            s = 2 * d + part

            @pl.when(d <= reach)
            def _():
                pltpu.make_async_copy(near[d - 1], slot(s), left_sems.at[s]).start()

            @pl.when(d > reach)
            def _():
                pltpu.make_async_copy(far[HALF - d - 1], slot(s), left_sems.at[s]).start()

    right[...] = jnp.zeros_like(right)
    inside = lax.broadcasted_iota(jnp.int32, (LANES, LANES), 0)
    for b in range(nb):
        pltpu.make_async_copy(rights[b], raw.at[b], raw_sems.at[b]).wait()
    blocks = 5

    @pl.loop(0, width // (LANES * blocks))
    def _(j):
        for i in range(blocks):
            at = pl.ds(pl.multiple_of((j * blocks + i) * LANES, LANES), LANES)
            for b in range(nb):
                chosen = jnp.where(inside == maps[b : b + 1, at], 1.0, 0.0).astype(jnp.bfloat16)
                right[pl.ds(b * LANES, rows), at] = jnp.dot(
                    raw[b, :, at], chosen, preferred_element_type=jnp.float32
                ).astype(jnp.bfloat16)

    for s in range(8):
        pltpu.make_async_copy(own, slot(s), left_sems.at[s]).wait()
    chunk = 1280
    for j in range(width // chunk):
        at = pl.ds(j * chunk, chunk)
        part = lax.dot_general(
            left[:, at], right[:, at], (((1,), (1,)), ((), ())), preferred_element_type=jnp.float32
        )
        total[...] = part if j == 0 else total[...] + part

    for s in range(8):
        d, other = s // 2, s % 2
        chip = jnp.where(core == 0, yy + HALF - d, yy + d) % HALF
        block = chip * CORES + jnp.where(other == 0, core, 1 - core)
        sums = []
        for b in range(nb):
            lanes = pl.ds(b * LANES, LANES)
            top = total[pl.ds(s * rows, half), lanes]
            low = total[pl.ds(s * rows + half, half), lanes]
            turned = jnp.concatenate(
                [low[:, half:rows], -low[:, :half], jnp.zeros((half, LANES - rows), jnp.float32)], axis=1
            )
            sums.append(top + turned)
        if has_rest:
            out[block] = scaled(jnp.concatenate([sums[0], rest[block, 0], rest[block, 1]], axis=0), rows)
        else:
            for b in range(nb):
                out[block, core ^ b] = sums[b]


def products(where, maps, lefts, rights, rest=None):
    nb = len(rights)
    rows, width = lefts[0].shape
    anywhere = pl.BlockSpec(memory_space=pl.ANY)
    vmem = pl.BlockSpec(memory_space=pltpu.VMEM)
    extra = [] if rest is None else [rest]
    return pl.pallas_call(
        functools.partial(products_kernel, nb, rest is not None),
        out_shape=jax.ShapeDtypeStruct((8, 3 * rows // 2, LANES), jnp.int16)
        if extra
        else jax.ShapeDtypeStruct((8, nb, rows // 2, LANES), jnp.float32),
        in_specs=[pl.BlockSpec(memory_space=pltpu.SMEM), vmem]
        + [anywhere] * (len(lefts) + nb)
        + [vmem] * len(extra),
        out_specs=vmem,
        scratch_shapes=[
            pltpu.VMEM((8 * rows, width), jnp.bfloat16),
            pltpu.VMEM((nb, rows, width), jnp.bfloat16),
            pltpu.VMEM((nb * LANES, width), jnp.bfloat16),
            pltpu.VMEM((8 * rows, nb * LANES), jnp.float32),
            pltpu.SemaphoreType.DMA((8,)),
            pltpu.SemaphoreType.DMA((nb,)),
        ],
        compiler_params=pltpu.CompilerParams(vmem_limit_bytes=40 * 2**20),
        cost_estimate=pl.CostEstimate(
            flops=2 * 8 * rows * nb * LANES * width,
            bytes_accessed=(8 + nb) * rows * width * 2,
            transcendentals=0,
        ),
    )(where, maps, *lefts, *rights, *extra)


def along_z(z, y, c):
    return z ^ (1 + c), y, c


def per_device(coeffs, shift_maps):
    bands, _, width = coeffs.shape
    position = lax.axis_index("ka")
    core = position & 1
    yy = (position >> 1) & (HALF - 1)
    where = jnp.stack([yy, core]).astype(jnp.int32)
    maps = lax.dynamic_index_in_dim(shift_maps, position >> 3, 0, keepdims=False) & (LANES - 1)
    later_maps = jnp.where(core == 0, maps[1:], jnp.stack([maps[2], maps[1]]))
    mine = coeffs.transpose(1, 0, 2).reshape(2 * bands, width)

    sibling = moved(mine, to_sibling)
    za = moved(mine, along_z)
    zb = moved(after(sibling, za), along_z)
    ga, gb, sa, sb = [mine], [sibling], [None], [None]
    for hops in range(1, HALF):
        deps = {1: [], 2: [], 3: [za, sa[1], sb[1]] if hops == 3 else []}[hops]
        ga.append(moved(after(ga[-1], *deps), along_y))
        gb.append(moved(gb[-1], along_y))
        sa.append(moved(ga[-1], to_sibling, wanted_from_sibling(hops)))
        sb.append(moved(gb[-1], to_sibling, wanted_from_sibling(hops)))
    opposite = moved(after(ga[-1], zb, sa[2], sb[2]), along_y)
    zs = moved(zb, to_sibling)
    lefts = [mine, sibling, *ga[1:], *gb[1:], *sa[1:], *sb[1:]]
    later = products(where, later_maps, lefts, [za, zs])
    every = products(where, maps[:1], lefts, [opposite], later)
    shares = lax.all_to_all(every, "ga", 0, 0, tiled=True)
    rows = 2 * bands
    units = jnp.exp2(shares[:, :, rows : rows + 1].astype(jnp.float32))
    total = (shares[:, :, :rows].astype(jnp.float32) * units).sum(axis=0).reshape(3, bands, rows)
    return total.transpose(1, 0, 2).reshape(bands, 3, 2, bands)


def solution(mesh):
    return jax.shard_map(
        per_device,
        mesh=mesh,
        in_specs=(P("ka", None, "ga"), P(None, None, "ga")),
        out_specs=P("ga", None, None, "ka"),
        check_vma=False,
    )
```

```python
import functools

import jax
import jax.numpy as jnp
from jax import lax
from jax.experimental import pallas as pl
from jax.experimental.pallas import tpu as pltpu
from jax.sharding import PartitionSpec as P

CORES = 2
YS = 8
HALF = YS // 2
LANES = 128


def place(i):
    return i // (YS * CORES), i // CORES % YS, i % CORES


def number(z, y, c):
    return (z * YS + y % YS) * CORES + c


def moved(shard, target, wanted=None):
    pairs = [(i, number(*target(*place(i)))) for i in range(lax.axis_size("ka"))]
    if wanted is not None:
        pairs = [(s, t) for s, t in pairs if wanted(*place(t))]
    return lax.ppermute(shard, "ka", pairs)


def to_sibling(z, y, c):
    return z, y, 1 - c


def along_y(z, y, c):
    return z, y + 1 - 2 * c, c


def wanted_from_sibling(hops):
    def wanted(z, y, c):
        return hops <= (HALF - 1 - y % HALF if c == 0 else y % HALF)

    return wanted


def after(shard, *others):
    return lax.optimization_barrier((shard, *others))[0]


def scaled(values, exponent_lane):
    most = jnp.max(jnp.abs(values), axis=1, keepdims=True)
    exponent = jnp.maximum(jnp.ceil(jnp.log2(jnp.maximum(most, 1e-30) / 32766.0)), -120.0)
    whole = jnp.round(values * jnp.exp2(-exponent))
    lane = lax.broadcasted_iota(jnp.int32, values.shape, 1)
    return jnp.where(lane == exponent_lane, exponent, whole).astype(jnp.int32).astype(jnp.int16)


def chosen_rows(shift, raw):
    inside = lax.broadcasted_iota(jnp.int32, (LANES, LANES), 0)
    chosen = jnp.where(inside == shift, 1.0, 0.0).astype(jnp.bfloat16)
    return jnp.dot(raw, chosen, preferred_element_type=jnp.float32).astype(jnp.bfloat16)


CHUNKS = 1


def products_kernel(nb, has_rest, *refs):
    refs = list(refs)
    where, maps, own, sibling = refs[:4]
    del refs[:4]
    ga, gb, sa, sb = (refs[3 * i : 3 * i + 3] for i in range(4))
    del refs[:12]
    rights = refs[:nb]
    del refs[:nb]
    rest = refs.pop(0) if has_rest else None
    out, left, raw, right, total, left_sems, raw_sems = refs
    rows, width = own.shape
    half = rows // 2
    chunk = width // CHUNKS
    yy, core = where[0], where[1]
    reach = jnp.where(core == 0, yy, HALF - 1 - yy)

    def copy(source, s, j):
        at = pl.ds(j * chunk, chunk)
        return pltpu.make_async_copy(
            source.at[:, at], left.at[pl.ds(s * rows, rows), at], left_sems.at[s, j]
        )

    for b in range(nb):
        pltpu.make_async_copy(rights[b], raw.at[b], raw_sems.at[b]).start()
    for j in range(CHUNKS):
        copy(own, 0, j).start()
        copy(sibling, 1, j).start()
        for d in range(1, HALF):
            for part, (near, far) in enumerate(((ga, sb), (gb, sa))):

                @pl.when(d <= reach)
                def _():
                    copy(near[d - 1], 2 * d + part, j).start()

                @pl.when(d > reach)
                def _():
                    copy(far[HALF - d - 1], 2 * d + part, j).start()

    spare = jnp.zeros((LANES - rows, width), jnp.bfloat16)
    for b in range(nb):
        right[pl.ds(b * LANES + rows, LANES - rows)] = spare
    for b in range(nb):
        pltpu.make_async_copy(rights[b], raw.at[b], raw_sems.at[b]).wait()
    for i in range(width // LANES):
        at = pl.ds(i * LANES, LANES)
        for b in range(nb):
            right[pl.ds(b * LANES, rows), at] = chosen_rows(maps[b : b + 1, at], raw[b, :, at])
    for j in range(CHUNKS):
        at = pl.ds(j * chunk, chunk)
        for s in range(8):
            copy(own, s, j).wait()
        part = lax.dot_general(
            left[:, at], right[:, at], (((1,), (1,)), ((), ())), preferred_element_type=jnp.float32
        )
        total[...] = part if j == 0 else total[...] + part

    if has_rest:
        out[:, pl.ds(0, rows)] = rest[...]
    for s in range(8):
        d, other = s // 2, s % 2
        chip = jnp.where(core == 0, yy + HALF - d, yy + d) % HALF
        block = chip * CORES + jnp.where(other == 0, core, 1 - core)
        sums = []
        for b in range(nb):
            lanes = pl.ds(b * LANES, LANES)
            top = total[pl.ds(s * rows, half), lanes]
            low = total[pl.ds(s * rows + half, half), lanes]
            turned = jnp.concatenate(
                [low[:, half:rows], -low[:, :half], jnp.zeros((half, LANES - rows), jnp.float32)], axis=1
            )
            sums.append(top + turned)
        if has_rest:
            spare_rows = jnp.zeros((64 - half, LANES), jnp.float32)
            out[block, pl.ds(rows, 64)] = scaled(jnp.concatenate([sums[0], spare_rows], axis=0), rows)
        else:
            first = jnp.where(core == 0, sums[0], sums[1])
            second = jnp.where(core == 0, sums[1], sums[0])
            out[block] = scaled(jnp.concatenate([first, second], axis=0), rows)


def products(where, maps, lefts, rights, rest=None):
    nb = len(rights)
    rows, width = lefts[0].shape
    anywhere = pl.BlockSpec(memory_space=pl.ANY)
    vmem = pl.BlockSpec(memory_space=pltpu.VMEM)
    extra = [] if rest is None else [rest]
    return pl.pallas_call(
        functools.partial(products_kernel, nb, rest is not None),
        out_shape=jax.ShapeDtypeStruct((8, rows + 64 if extra else rows, LANES), jnp.int16),
        in_specs=[pl.BlockSpec(memory_space=pltpu.SMEM), vmem]
        + [anywhere] * (len(lefts) + nb)
        + [vmem] * len(extra),
        out_specs=vmem,
        scratch_shapes=[
            pltpu.VMEM((8 * rows, width), jnp.bfloat16),
            pltpu.VMEM((nb, rows, width), jnp.bfloat16),
            pltpu.VMEM((nb * LANES, width), jnp.bfloat16),
            pltpu.VMEM((8 * rows, nb * LANES), jnp.float32),
            pltpu.SemaphoreType.DMA((8, CHUNKS)),
            pltpu.SemaphoreType.DMA((nb,)),
        ],
        compiler_params=pltpu.CompilerParams(vmem_limit_bytes=40 * 2**20),
        cost_estimate=pl.CostEstimate(
            flops=2 * 8 * rows * nb * LANES * width,
            bytes_accessed=(8 + nb) * rows * width * 2,
            transcendentals=0,
        ),
    )(where, maps, *lefts, *rights, *extra)


def along_z(z, y, c):
    return z ^ (1 + c), y, c


def per_device(coeffs, shift_maps):
    bands, _, width = coeffs.shape
    position = lax.axis_index("ka")
    core = position & 1
    yy = (position >> 1) & (HALF - 1)
    where = jnp.stack([yy, core]).astype(jnp.int32)
    maps = lax.dynamic_index_in_dim(shift_maps, position >> 3, 0, keepdims=False) & (LANES - 1)
    later_maps = jnp.where(core == 0, maps[1:], jnp.stack([maps[2], maps[1]]))
    mine = coeffs.transpose(1, 0, 2).reshape(2 * bands, width)

    sibling = moved(mine, to_sibling)
    za = moved(mine, along_z)
    zb = moved(after(sibling, za), along_z)
    ga, gb, sa, sb = [mine], [sibling], [None], [None]
    for hops in range(1, HALF):
        deps = {1: [], 2: [], 3: [za, sa[1], sb[1]] if hops == 3 else []}[hops]
        ga.append(moved(after(ga[-1], *deps), along_y))
        gb.append(moved(gb[-1], along_y))
        sa.append(moved(ga[-1], to_sibling, wanted_from_sibling(hops)))
        sb.append(moved(gb[-1], to_sibling, wanted_from_sibling(hops)))
    opposite = moved(after(ga[-1], zb, sa[2], sb[2]), along_y)
    zs = moved(zb, to_sibling)
    lefts = [mine, sibling, *ga[1:], *gb[1:], *sa[1:], *sb[1:]]
    later = products(where, later_maps, lefts, [za, zs])
    every = products(where, maps[:1], lefts, [opposite], later)
    shares = lax.all_to_all(every, "ga", 0, 0, tiled=True)
    rows = 2 * bands
    units = jnp.exp2(shares[:, : 3 * bands, rows : rows + 1].astype(jnp.float32))
    total = (shares[:, : 3 * bands, :rows].astype(jnp.float32) * units).sum(axis=0)
    second, third, first = total[:bands], total[bands:rows], total[rows:]
    return jnp.stack([first, second, third], axis=1).reshape(bands, 3, 2, bands)


def solution(mesh):
    return jax.shard_map(
        per_device,
        mesh=mesh,
        in_specs=(P("ka", None, "ga"), P(None, None, "ga")),
        out_specs=P("ga", None, None, "ka"),
        check_vma=False,
    )
```

```python
import functools

import jax
import jax.numpy as jnp
from jax import lax
from jax.experimental import pallas as pl
from jax.experimental.pallas import tpu as pltpu
from jax.sharding import PartitionSpec as P

CORES = 2
YS = 8
HALF = YS // 2
LANES = 128


def place(i):
    return i // (YS * CORES), i // CORES % YS, i % CORES


def number(z, y, c):
    return (z * YS + y % YS) * CORES + c


def moved(shard, target, wanted=None):
    pairs = [(i, number(*target(*place(i)))) for i in range(lax.axis_size("ka"))]
    if wanted is not None:
        pairs = [(s, t) for s, t in pairs if wanted(*place(t))]
    return lax.ppermute(shard, "ka", pairs)


def to_sibling(z, y, c):
    return z, y, 1 - c


def along_y(z, y, c):
    return z, y + 1 - 2 * c, c


def wanted_from_sibling(hops):
    def wanted(z, y, c):
        return hops <= (HALF - 1 - y % HALF if c == 0 else y % HALF)

    return wanted


def after(shard, *others):
    return lax.optimization_barrier((shard, *others))[0]


def scaled(values, exponent_lane):
    most = jnp.max(jnp.abs(values), axis=1, keepdims=True)
    exponent = jnp.maximum(jnp.ceil(jnp.log2(jnp.maximum(most, 1e-30) / 32766.0)), -120.0)
    whole = jnp.round(values * jnp.exp2(-exponent))
    lane = lax.broadcasted_iota(jnp.int32, values.shape, 1)
    return jnp.where(lane == exponent_lane, exponent, whole).astype(jnp.int32).astype(jnp.int16)


def chosen_rows(shift, raw):
    inside = lax.broadcasted_iota(jnp.int32, (LANES, LANES), 0)
    chosen = jnp.where(inside == shift, 1.0, 0.0).astype(jnp.bfloat16)
    return jnp.dot(raw, chosen, preferred_element_type=jnp.float32).astype(jnp.bfloat16)


def signed(sums, half):
    rows = 2 * half
    low = sums[half:]
    spare = jnp.zeros((half, LANES - rows), jnp.float32)
    return sums[:half] + jnp.concatenate([low[:, half:rows], -low[:, :half], spare], axis=1)


def products_kernel(nb, *refs):
    refs = list(refs)
    where, maps = refs[:2]
    del refs[:2]
    yy, core = where[0], where[1]
    reach = jnp.where(core == 0, yy, HALF - 1 - yy)
    if nb == 2:
        own, sibling = refs[:2]
        ga, gb, sa, sb = (refs[2 + 3 * i : 5 + 3 * i] for i in range(4))
        rights = refs[14:16]
        out, left, raw, right, total, raw_sems, left_sems = refs[16:]
    else:
        left, done, *rights = refs[:3]
        out, raw, right, total, raw_sems = refs[3:]
    rows, width = raw.shape[1:]
    half = rows // 2

    def copy(source, s):
        return pltpu.make_async_copy(source, left.at[pl.ds(s * rows, rows)], left_sems.at[s])

    for b in range(nb):
        pltpu.make_async_copy(rights[b], raw.at[b], raw_sems.at[b]).start()
    if nb == 2:
        copy(own, 0).start()
        copy(sibling, 1).start()
        for d in range(1, HALF):
            for part, (near, far) in enumerate(((ga, sb), (gb, sa))):

                @pl.when(d <= reach)
                def _():
                    copy(near[d - 1], 2 * d + part).start()

                @pl.when(d > reach)
                def _():
                    copy(far[HALF - d - 1], 2 * d + part).start()

    spare = jnp.zeros((LANES - rows, width), jnp.bfloat16)
    for b in range(nb):
        right[pl.ds(b * LANES + rows, LANES - rows)] = spare
    for b in range(nb):
        pltpu.make_async_copy(rights[b], raw.at[b], raw_sems.at[b]).wait()
    for i in range(width // LANES):
        at = pl.ds(i * LANES, LANES)
        for b in range(nb):
            right[pl.ds(b * LANES, rows), at] = chosen_rows(maps[b : b + 1, at], raw[b, :, at])
    if nb == 2:
        for s in range(8):
            copy(own, s).wait()
    total[...] = lax.dot_general(
        left[...], right[...], (((1,), (1,)), ((), ())), preferred_element_type=jnp.float32
    )
    if nb == 1:
        out[:, pl.ds(0, rows)] = done[...]
    for s in range(8):
        d, other = s // 2, s % 2
        chip = jnp.where(core == 0, yy + HALF - d, yy + d) % HALF
        block = chip * CORES + jnp.where(other == 0, core, 1 - core)
        sums = [signed(total[pl.ds(s * rows, rows), pl.ds(b * LANES, LANES)], half) for b in range(nb)]
        if nb == 1:
            spare_rows = jnp.zeros((64 - half, LANES), jnp.float32)
            out[block, pl.ds(rows, 64)] = scaled(jnp.concatenate([sums[0], spare_rows], axis=0), rows)
        else:
            first = jnp.where(core == 0, sums[0], sums[1])
            second = jnp.where(core == 0, sums[1], sums[0])
            out[block] = scaled(jnp.concatenate([first, second], axis=0), rows)


def products(where, maps, bands, rights):
    nb = len(rights)
    rows, width = rights[0].shape
    anywhere = pl.BlockSpec(memory_space=pl.ANY)
    vmem = pl.BlockSpec(memory_space=pltpu.VMEM)
    scratch = [
        pltpu.VMEM((nb, rows, width), jnp.bfloat16),
        pltpu.VMEM((nb * LANES, width), jnp.bfloat16),
        pltpu.VMEM((8 * rows, nb * LANES), jnp.float32),
        pltpu.SemaphoreType.DMA((nb,)),
    ]
    if nb == 2:
        outs = (
            jax.ShapeDtypeStruct((8, rows, LANES), jnp.int16),
            pltpu.VMEM((8 * rows, width), jnp.bfloat16),
        )
        scratch.append(pltpu.SemaphoreType.DMA((8,)))
    else:
        outs = jax.ShapeDtypeStruct((8, rows + 64, LANES), jnp.int16)
    return pl.pallas_call(
        functools.partial(products_kernel, nb),
        out_shape=outs,
        in_specs=[pl.BlockSpec(memory_space=pltpu.SMEM), vmem]
        + [anywhere if nb == 2 else vmem] * len(bands)
        + [anywhere] * nb,
        out_specs=(vmem, vmem) if nb == 2 else vmem,
        scratch_shapes=scratch,
        compiler_params=pltpu.CompilerParams(vmem_limit_bytes=24 * 2**20),
        cost_estimate=pl.CostEstimate(
            flops=2 * 8 * rows * nb * LANES * width,
            bytes_accessed=(8 + nb) * rows * width * 2,
            transcendentals=0,
        ),
    )(where, maps, *bands, *rights)


def along_z(z, y, c):
    return z ^ (1 + c), y, c


def per_device(coeffs, shift_maps):
    bands, _, width = coeffs.shape
    position = lax.axis_index("ka")
    core = position & 1
    yy = (position >> 1) & (HALF - 1)
    where = jnp.stack([yy, core]).astype(jnp.int32)
    maps = lax.dynamic_index_in_dim(shift_maps, position >> 3, 0, keepdims=False) & (LANES - 1)
    later_maps = jnp.where(core == 0, maps[1:], jnp.stack([maps[2], maps[1]]))
    mine = coeffs.transpose(1, 0, 2).reshape(2 * bands, width)

    sibling = moved(mine, to_sibling)
    za = moved(mine, along_z)
    zb = moved(after(sibling, za), along_z)
    ga, gb, sa, sb = [mine], [sibling], [None], [None]
    for hops in range(1, HALF):
        deps = {1: [], 2: [], 3: [za, sa[1], sb[1]] if hops == 3 else []}[hops]
        ga.append(moved(after(ga[-1], *deps), along_y))
        gb.append(moved(gb[-1], along_y))
        sa.append(moved(ga[-1], to_sibling, wanted_from_sibling(hops)))
        sb.append(moved(gb[-1], to_sibling, wanted_from_sibling(hops)))
    opposite = moved(after(ga[-1], zb, sa[2], sb[2]), along_y)
    zs = moved(zb, to_sibling)
    lefts = [mine, sibling, *ga[1:], *gb[1:], *sa[1:], *sb[1:]]
    later, packed = products(where, later_maps, lefts, [za, zs])
    every = products(where, maps[:1], [packed, later], [opposite])
    shares = lax.all_to_all(every, "ga", 0, 0, tiled=True)
    rows = 2 * bands
    units = jnp.exp2(shares[:, : 3 * bands, rows : rows + 1].astype(jnp.float32))
    total = (shares[:, : 3 * bands, :rows].astype(jnp.float32) * units).sum(axis=0)
    second, third, first = total[:bands], total[bands:rows], total[rows:]
    return jnp.stack([first, second, third], axis=1).reshape(bands, 3, 2, bands)


def solution(mesh):
    return jax.shard_map(
        per_device,
        mesh=mesh,
        in_specs=(P("ka", None, "ga"), P(None, None, "ga")),
        out_specs=P("ga", None, None, "ka"),
        check_vma=False,
    )
```

```python
import functools

import jax
import jax.numpy as jnp
from jax import lax
from jax.experimental import pallas as pl
from jax.experimental.pallas import tpu as pltpu
from jax.sharding import PartitionSpec as P

CORES = 2
YS = 8
HALF = YS // 2
LANES = 128


def place(i):
    return i // (YS * CORES), i // CORES % YS, i % CORES


def number(z, y, c):
    return (z * YS + y % YS) * CORES + c


def moved(shard, target, wanted=None):
    pairs = [(i, number(*target(*place(i)))) for i in range(lax.axis_size("ka"))]
    if wanted is not None:
        pairs = [(s, t) for s, t in pairs if wanted(*place(t))]
    return lax.ppermute(shard, "ka", pairs)


def to_sibling(z, y, c):
    return z, y, 1 - c


def along_y(z, y, c):
    return z, y + 1 - 2 * c, c


def wanted_from_sibling(hops):
    def wanted(z, y, c):
        return hops <= (HALF - 1 - y % HALF if c == 0 else y % HALF)

    return wanted


def after(shard, *others):
    return lax.optimization_barrier((shard, *others))[0]


def scaled(values, exponent_lane):
    most = jnp.max(jnp.abs(values), axis=1, keepdims=True)
    exponent = jnp.maximum(jnp.ceil(jnp.log2(jnp.maximum(most, 1e-30) / 32766.0)), -120.0)
    whole = jnp.round(values * jnp.exp2(-exponent))
    lane = lax.broadcasted_iota(jnp.int32, values.shape, 1)
    return jnp.where(lane == exponent_lane, exponent, whole).astype(jnp.int32).astype(jnp.int16)


def chosen_rows(shift, raw):
    inside = lax.broadcasted_iota(jnp.int32, (LANES, LANES), 0)
    chosen = jnp.where(inside == shift, 1.0, 0.0).astype(jnp.bfloat16)
    return jnp.dot(raw, chosen, preferred_element_type=jnp.float32).astype(jnp.bfloat16)


def signed(sums, half):
    rows = 2 * half
    low = sums[half:]
    spare = jnp.zeros((half, LANES - rows), jnp.float32)
    return sums[:half] + jnp.concatenate([low[:, half:rows], -low[:, :half], spare], axis=1)


def products_kernel(nb, *refs):
    refs = list(refs)
    where, maps = refs[:2]
    del refs[:2]
    yy, core = where[0], where[1]
    reach = jnp.where(core == 0, yy, HALF - 1 - yy)
    if nb == 2:
        own, sibling = refs[:2]
        ga, gb, sa, sb = (refs[2 + 3 * i : 5 + 3 * i] for i in range(4))
        rights = refs[14:16]
        out, left, raw, right, total, raw_sems, left_sems = refs[16:]
    else:
        left, done, *rights = refs[:3]
        out, raw, right, total, raw_sems = refs[3:]
    rows, width = raw.shape[1:]
    half = rows // 2

    def copy(source, s):
        return pltpu.make_async_copy(source, left.at[pl.ds(s * rows, rows)], left_sems.at[s])

    for b in range(nb):
        pltpu.make_async_copy(rights[b], raw.at[b], raw_sems.at[b]).start()
    if nb == 2:
        copy(own, 0).start()
        copy(sibling, 1).start()
        for d in range(1, HALF):
            for part, (near, far) in enumerate(((ga, sb), (gb, sa))):

                @pl.when(d <= reach)
                def _():
                    copy(near[d - 1], 2 * d + part).start()

                @pl.when(d > reach)
                def _():
                    copy(far[HALF - d - 1], 2 * d + part).start()

    spare = jnp.zeros((LANES - rows, width), jnp.bfloat16)
    for b in range(nb):
        right[pl.ds(b * LANES + rows, LANES - rows)] = spare
    for b in range(nb):
        pltpu.make_async_copy(rights[b], raw.at[b], raw_sems.at[b]).wait()
    for i in range(width // LANES):
        at = pl.ds(i * LANES, LANES)
        for b in range(nb):
            right[pl.ds(b * LANES, rows), at] = chosen_rows(maps[b : b + 1, at], raw[b, :, at])
    if nb == 2:
        for s in range(8):
            copy(own, s).wait()
    total[...] = lax.dot_general(
        left[...], right[...], (((1,), (1,)), ((), ())), preferred_element_type=jnp.float32
    )
    if nb == 1:
        out[:, pl.ds(0, rows)] = done[...]
    for s in range(8):
        d, other = s // 2, s % 2
        chip = jnp.where(core == 0, yy + HALF - d, yy + d) & (HALF - 1)
        block = (((chip & 1) << 1) | (core ^ other)) << 1 | (chip >> 1)
        sums = [signed(total[pl.ds(s * rows, rows), pl.ds(b * LANES, LANES)], half) for b in range(nb)]
        if nb == 1:
            spare_rows = jnp.zeros((64 - half, LANES), jnp.float32)
            out[block, pl.ds(rows, 64)] = scaled(jnp.concatenate([sums[0], spare_rows], axis=0), rows)
        else:
            first = jnp.where(core == 0, sums[0], sums[1])
            second = jnp.where(core == 0, sums[1], sums[0])
            out[block] = scaled(jnp.concatenate([first, second], axis=0), rows)


def products(where, maps, bands, rights):
    nb = len(rights)
    rows, width = rights[0].shape
    anywhere = pl.BlockSpec(memory_space=pl.ANY)
    vmem = pl.BlockSpec(memory_space=pltpu.VMEM)
    scratch = [
        pltpu.VMEM((nb, rows, width), jnp.bfloat16),
        pltpu.VMEM((nb * LANES, width), jnp.bfloat16),
        pltpu.VMEM((8 * rows, nb * LANES), jnp.float32),
        pltpu.SemaphoreType.DMA((nb,)),
    ]
    if nb == 2:
        outs = (
            jax.ShapeDtypeStruct((8, rows, LANES), jnp.int16),
            pltpu.VMEM((8 * rows, width), jnp.bfloat16),
        )
        scratch.append(pltpu.SemaphoreType.DMA((8,)))
    else:
        outs = jax.ShapeDtypeStruct((8, rows + 64, LANES), jnp.int16)
    return pl.pallas_call(
        functools.partial(products_kernel, nb),
        out_shape=outs,
        in_specs=[pl.BlockSpec(memory_space=pltpu.SMEM), vmem]
        + [anywhere if nb == 2 else vmem] * len(bands)
        + [anywhere] * nb,
        out_specs=(vmem, vmem) if nb == 2 else vmem,
        scratch_shapes=scratch,
        compiler_params=pltpu.CompilerParams(vmem_limit_bytes=24 * 2**20),
        cost_estimate=pl.CostEstimate(
            flops=2 * 8 * rows * nb * LANES * width,
            bytes_accessed=(8 + nb) * rows * width * 2,
            transcendentals=0,
        ),
    )(where, maps, *bands, *rights)


def along_z(z, y, c):
    return z ^ (1 + c), y, c


def per_device(coeffs, shift_maps):
    bands, _, width = coeffs.shape
    position = lax.axis_index("ka")
    core = position & 1
    yy = (position >> 1) & (HALF - 1)
    where = jnp.stack([yy, core]).astype(jnp.int32)
    maps = lax.dynamic_index_in_dim(shift_maps, position >> 3, 0, keepdims=False) & (LANES - 1)
    later_maps = jnp.where(core == 0, maps[1:], jnp.stack([maps[2], maps[1]]))
    mine = coeffs.transpose(1, 0, 2).reshape(2 * bands, width)

    sibling = moved(mine, to_sibling)
    za = moved(mine, along_z)
    zb = moved(after(sibling, za), along_z)
    ga, gb, sa, sb = [mine], [sibling], [None], [None]
    for hops in range(1, HALF):
        ga.append(moved(after(ga[-1], za, sa[1], sb[1]) if hops == 3 else ga[-1], along_y))
        gb.append(moved(gb[-1], along_y))
        sa.append(moved(ga[-1], to_sibling, wanted_from_sibling(hops)))
        sb.append(moved(gb[-1], to_sibling, wanted_from_sibling(hops)))
    opposite = moved(after(ga[-1], zb, sa[2], sb[2]), along_y)
    zs = moved(zb, to_sibling)
    lefts = [mine, sibling, *ga[1:], *gb[1:], *sa[1:], *sb[1:]]
    later, packed = products(where, later_maps, lefts, [za, zs])
    every = products(where, maps[:1], [packed, later], [opposite])
    shares = lax.all_to_all(
        every, "ga", 0, 0, axis_index_groups=[[0, 1, 2, 3], [4, 5, 6, 7]], tiled=True
    )
    rows = 2 * bands
    units = jnp.exp2(shares[:, : 3 * bands, rows : rows + 1].astype(jnp.float32))
    sums = shares[:, : 3 * bands, :rows].astype(jnp.float32) * units
    lower, upper = sums[0::2].sum(axis=0), sums[1::2].sum(axis=0)
    low = lax.axis_index("ga") < 4
    theirs = lax.ppermute(jnp.where(low, upper, lower), "ga", [(g, g ^ 4) for g in range(8)])
    total = jnp.where(low, lower, upper) + theirs
    second, third, first = total[:bands], total[bands:rows], total[rows:]
    return jnp.stack([first, second, third], axis=1).reshape(bands, 3, 2, bands)


def solution(mesh):
    return jax.shard_map(
        per_device,
        mesh=mesh,
        in_specs=(P("ka", None, "ga"), P(None, None, "ga")),
        out_specs=P("ga", None, None, "ka"),
        check_vma=False,
    )
```

```python
import functools
import math

import jax
import jax.numpy as jnp
from jax import lax
from jax.experimental import pallas as pl
from jax.experimental.pallas import tpu as pltpu
from jax.sharding import PartitionSpec as P

CORES = 2
YS = 8
HALF = YS // 2
LANES = 128


def place(i):
    return i // (YS * CORES), i // CORES % YS, i % CORES


def number(z, y, c):
    return (z * YS + y % YS) * CORES + c


def moved(shard, target, wanted=None):
    pairs = [(i, number(*target(*place(i)))) for i in range(lax.axis_size("ka"))]
    if wanted is not None:
        pairs = [(s, t) for s, t in pairs if wanted(*place(t))]
    return lax.ppermute(shard, "ka", pairs)


def to_sibling(z, y, c):
    return z, y, 1 - c


def along_y(z, y, c):
    return z, y + 1 - 2 * c, c


def wanted_from_sibling(hops):
    def wanted(z, y, c):
        return hops <= (HALF - 1 - y % HALF if c == 0 else y % HALF)

    return wanted


def after(shard, *others):
    return lax.optimization_barrier((shard, *others))[0]


def scaled(values, exponent_lane):
    most = jnp.max(jnp.abs(values), axis=1, keepdims=True)
    exponent = jnp.maximum(jnp.ceil(jnp.log2(jnp.maximum(most, 1e-36)) - math.log2(32700)), -126.0)
    whole = jnp.round(values * jnp.exp2(-exponent))
    lane = lax.broadcasted_iota(jnp.int32, values.shape, 1)
    return jnp.where(lane == exponent_lane, exponent, whole).astype(jnp.int32).astype(jnp.int16)


def chosen_rows(shift, raw):
    inside = lax.broadcasted_iota(jnp.int32, (LANES, LANES), 0)
    chosen = jnp.where(inside == shift, 1.0, 0.0).astype(jnp.bfloat16)
    return jnp.dot(raw, chosen, preferred_element_type=jnp.float32).astype(jnp.bfloat16)


def signed(sums, half):
    rows = 2 * half
    low = sums[half:]
    spare = jnp.zeros((half, LANES - rows), jnp.float32)
    return sums[:half] + jnp.concatenate([low[:, half:rows], -low[:, :half], spare], axis=1)


def products_kernel(nb, *refs):
    refs = list(refs)
    where, maps = refs[:2]
    del refs[:2]
    yy, core = where[0], where[1]
    reach = jnp.where(core == 0, yy, HALF - 1 - yy)
    if nb == 2:
        own, sibling = refs[:2]
        ga, gb, sa, sb = (refs[2 + 3 * i : 5 + 3 * i] for i in range(4))
        rights = refs[14:16]
        out, left, raw, right, total, raw_sems, left_sems = refs[16:]
    else:
        left, done, *rights = refs[:3]
        out, raw, right, total, raw_sems = refs[3:]
    rows, width = raw.shape[1:]
    half = rows // 2

    def copy(source, s):
        return pltpu.make_async_copy(source, left.at[pl.ds(s * rows, rows)], left_sems.at[s])

    for b in range(nb):
        pltpu.make_async_copy(rights[b], raw.at[b], raw_sems.at[b]).start()
    if nb == 2:
        copy(own, 0).start()
        copy(sibling, 1).start()
        for d in range(1, HALF):
            for part, (near, far) in enumerate(((ga, sb), (gb, sa))):

                @pl.when(d <= reach)
                def _():
                    copy(near[d - 1], 2 * d + part).start()

                @pl.when(d > reach)
                def _():
                    copy(far[HALF - d - 1], 2 * d + part).start()

    spare = jnp.zeros((LANES - rows, width), jnp.bfloat16)
    for b in range(nb):
        right[pl.ds(b * LANES + rows, LANES - rows)] = spare
    for b in range(nb):
        pltpu.make_async_copy(rights[b], raw.at[b], raw_sems.at[b]).wait()
    for i in range(width // LANES):
        at = pl.ds(i * LANES, LANES)
        for b in range(nb):
            right[pl.ds(b * LANES, rows), at] = chosen_rows(maps[b : b + 1, at], raw[b, :, at])
    if nb == 2:
        for s in range(8):
            copy(own, s).wait()
    total[...] = lax.dot_general(
        left[...], right[...], (((1,), (1,)), ((), ())), preferred_element_type=jnp.float32
    )
    if nb == 1:
        out[:, pl.ds(0, rows)] = done[...]
    for s in range(8):
        d, other = s // 2, s % 2
        chip = jnp.where(core == 0, yy + HALF - d, yy + d) & (HALF - 1)
        block = (((chip & 1) << 1) | (core ^ other)) << 1 | (chip >> 1)
        sums = [signed(total[pl.ds(s * rows, rows), pl.ds(b * LANES, LANES)], half) for b in range(nb)]
        if nb == 1:
            spare_rows = jnp.zeros((64 - half, LANES), jnp.float32)
            out[block, pl.ds(rows, 64)] = scaled(jnp.concatenate([sums[0], spare_rows], axis=0), rows)
        else:
            first = jnp.where(core == 0, sums[0], sums[1])
            second = jnp.where(core == 0, sums[1], sums[0])
            out[block] = scaled(jnp.concatenate([first, second], axis=0), rows)


def products(where, maps, bands, rights):
    nb = len(rights)
    rows, width = rights[0].shape
    anywhere = pl.BlockSpec(memory_space=pl.ANY)
    vmem = pl.BlockSpec(memory_space=pltpu.VMEM)
    scratch = [
        pltpu.VMEM((nb, rows, width), jnp.bfloat16),
        pltpu.VMEM((nb * LANES, width), jnp.bfloat16),
        pltpu.VMEM((8 * rows, nb * LANES), jnp.float32),
        pltpu.SemaphoreType.DMA((nb,)),
    ]
    if nb == 2:
        outs = (
            jax.ShapeDtypeStruct((8, rows, LANES), jnp.int16),
            pltpu.VMEM((8 * rows, width), jnp.bfloat16),
        )
        scratch.append(pltpu.SemaphoreType.DMA((8,)))
    else:
        outs = jax.ShapeDtypeStruct((8, rows + 64, LANES), jnp.int16)
    return pl.pallas_call(
        functools.partial(products_kernel, nb),
        out_shape=outs,
        in_specs=[pl.BlockSpec(memory_space=pltpu.SMEM), vmem]
        + [anywhere if nb == 2 else vmem] * len(bands)
        + [anywhere] * nb,
        out_specs=(vmem, vmem) if nb == 2 else vmem,
        scratch_shapes=scratch,
        compiler_params=pltpu.CompilerParams(vmem_limit_bytes=24 * 2**20),
        cost_estimate=pl.CostEstimate(
            flops=2 * 8 * rows * nb * LANES * width,
            bytes_accessed=(8 + nb) * rows * width * 2,
            transcendentals=0,
        ),
    )(where, maps, *bands, *rights)


def along_z(z, y, c):
    return z ^ (1 + c), y, c


def per_device(coeffs, shift_maps):
    bands, _, width = coeffs.shape
    position = lax.axis_index("ka")
    core = position & 1
    yy = (position >> 1) & (HALF - 1)
    where = jnp.stack([yy, core]).astype(jnp.int32)
    maps = lax.dynamic_index_in_dim(shift_maps, position >> 3, 0, keepdims=False) & (LANES - 1)
    later_maps = jnp.where(core == 0, maps[1:], jnp.stack([maps[2], maps[1]]))
    mine = coeffs.transpose(1, 0, 2).reshape(2 * bands, width)

    sibling = moved(mine, to_sibling)
    za = moved(mine, along_z)
    zb = moved(after(sibling, za), along_z)
    ga, gb, sa, sb = [mine], [sibling], [None], [None]
    for hops in range(1, HALF):
        ga.append(moved(after(ga[-1], za, sa[1], sb[1]) if hops == 3 else ga[-1], along_y))
        gb.append(moved(gb[-1], along_y))
        sa.append(moved(ga[-1], to_sibling, wanted_from_sibling(hops)))
        sb.append(moved(gb[-1], to_sibling, wanted_from_sibling(hops)))
    opposite = moved(after(ga[-1], zb, sa[2], sb[2]), along_y)
    zs = moved(zb, to_sibling)
    lefts = [mine, sibling, *ga[1:], *gb[1:], *sa[1:], *sb[1:]]
    later, packed = products(where, later_maps, lefts, [za, zs])
    every = products(where, maps[:1], [packed, later], [opposite])
    shares = lax.all_to_all(
        every, "ga", 0, 0, axis_index_groups=[[0, 1, 2, 3], [4, 5, 6, 7]], tiled=True
    )
    rows = 2 * bands
    units = jnp.exp2(shares[:, : 3 * bands, rows : rows + 1].astype(jnp.float32))
    sums = shares[:, : 3 * bands, :rows].astype(jnp.float32) * units
    lower, upper = sums[0::2].sum(axis=0), sums[1::2].sum(axis=0)
    low = lax.axis_index("ga") < 4
    theirs = lax.ppermute(jnp.where(low, upper, lower), "ga", [(g, g ^ 4) for g in range(8)])
    total = jnp.where(low, lower, upper) + theirs
    second, third, first = total[:bands], total[bands:rows], total[rows:]
    return jnp.stack([first, second, third], axis=1).reshape(bands, 3, 2, bands)


def solution(mesh):
    return jax.shard_map(
        per_device,
        mesh=mesh,
        in_specs=(P("ka", None, "ga"), P(None, None, "ga")),
        out_specs=P("ga", None, None, "ka"),
        check_vma=False,
    )
```

```python
import functools
import math

import jax
import jax.numpy as jnp
from jax import lax
from jax.experimental import pallas as pl
from jax.experimental.pallas import tpu as pltpu
from jax.sharding import PartitionSpec as P

CORES = 2
YS = 8
HALF = YS // 2
LANES = 128


def place(i):
    return i // (YS * CORES), i // CORES % YS, i % CORES


def number(z, y, c):
    return (z * YS + y % YS) * CORES + c


def moved(shard, target, wanted=None):
    pairs = [(i, number(*target(*place(i)))) for i in range(lax.axis_size("ka"))]
    if wanted is not None:
        pairs = [(s, t) for s, t in pairs if wanted(*place(t))]
    return lax.ppermute(shard, "ka", pairs)


def to_sibling(z, y, c):
    return z, y, 1 - c


def along_y(z, y, c):
    return z, y + 1 - 2 * c, c


def wanted_from_sibling(hops):
    def wanted(z, y, c):
        return hops <= (HALF - 1 - y % HALF if c == 0 else y % HALF)

    return wanted


def after(shard, *others):
    return lax.optimization_barrier((shard, *others))[0]


def scaled(values, exponent_lane):
    most = jnp.max(jnp.abs(values), axis=1, keepdims=True)
    exponent = jnp.maximum(jnp.ceil(jnp.log2(jnp.maximum(most, 1e-36)) - math.log2(32700)), -126.0)
    whole = jnp.round(values * jnp.exp2(-exponent))
    lane = lax.broadcasted_iota(jnp.int32, values.shape, 1)
    return jnp.where(lane == exponent_lane, exponent, whole).astype(jnp.int32).astype(jnp.int16)


def chosen_rows(shift, raw):
    inside = lax.broadcasted_iota(jnp.int32, (LANES, LANES), 0)
    chosen = jnp.where(inside == shift, 1.0, 0.0).astype(jnp.bfloat16)
    return jnp.dot(raw, chosen, preferred_element_type=jnp.float32).astype(jnp.bfloat16)


def signed(sums, half):
    rows = 2 * half
    low = sums[half:]
    spare = jnp.zeros((half, LANES - rows), jnp.float32)
    return sums[:half] + jnp.concatenate([low[:, half:rows], -low[:, :half], spare], axis=1)


def products_kernel(nb, *refs):
    refs = list(refs)
    where, maps = refs[:2]
    del refs[:2]
    yy, core = where[0], where[1]
    reach = jnp.where(core == 0, yy, HALF - 1 - yy)
    if nb == 2:
        own, sibling = refs[:2]
        ga, gb, sa, sb = (refs[2 + 3 * i : 5 + 3 * i] for i in range(4))
        rights = refs[14:16]
        out, left, raw, right, total, raw_sems, left_sems = refs[16:]
    else:
        left, done, *rights = refs[:3]
        out, raw, right, total, raw_sems = refs[3:]
    rows, width = raw.shape[1:]
    half = rows // 2

    def copy(source, s):
        return pltpu.make_async_copy(source, left.at[pl.ds(s * rows, rows)], left_sems.at[s])

    for b in range(nb):
        pltpu.make_async_copy(rights[b], raw.at[b], raw_sems.at[b]).start()
    if nb == 2:
        copy(own, 0).start()
        copy(sibling, 1).start()
        for d in range(1, HALF):
            for part, (near, far) in enumerate(((ga, sb), (gb, sa))):

                @pl.when(d <= reach)
                def _():
                    copy(near[d - 1], 2 * d + part).start()

                @pl.when(d > reach)
                def _():
                    copy(far[HALF - d - 1], 2 * d + part).start()

    spare = jnp.zeros((LANES - rows, width), jnp.bfloat16)
    for b in range(nb):
        right[pl.ds(b * LANES + rows, LANES - rows)] = spare
    for b in range(nb):
        pltpu.make_async_copy(rights[b], raw.at[b], raw_sems.at[b]).wait()
    for i in range(width // LANES):
        at = pl.ds(i * LANES, LANES)
        for b in range(nb):
            right[pl.ds(b * LANES, rows), at] = chosen_rows(maps[b : b + 1, at], raw[b, :, at])
    if nb == 2:
        for s in range(8):
            copy(own, s).wait()
    total[...] = lax.dot_general(
        left[...], right[...], (((1,), (1,)), ((), ())), preferred_element_type=jnp.float32
    )
    if nb == 1:
        out[:, pl.ds(0, rows)] = done[...]
    for s in range(8):
        d, other = s // 2, s % 2
        chip = jnp.where(core == 0, yy + HALF - d, yy + d) & (HALF - 1)
        block = (((chip & 1) << 1) | (core ^ other)) << 1 | (chip >> 1)
        sums = [signed(total[pl.ds(s * rows, rows), pl.ds(b * LANES, LANES)], half) for b in range(nb)]
        if nb == 1:
            spare_rows = jnp.zeros((64 - half, LANES), jnp.float32)
            out[block, pl.ds(rows, 64)] = scaled(jnp.concatenate([sums[0], spare_rows], axis=0), rows)
        else:
            first = jnp.where(core == 0, sums[0], sums[1])
            second = jnp.where(core == 0, sums[1], sums[0])
            out[block] = scaled(jnp.concatenate([first, second], axis=0), rows)


def products(where, maps, bands, rights):
    nb = len(rights)
    rows, width = rights[0].shape
    anywhere = pl.BlockSpec(memory_space=pl.ANY)
    vmem = pl.BlockSpec(memory_space=pltpu.VMEM)
    scratch = [
        pltpu.VMEM((nb, rows, width), jnp.bfloat16),
        pltpu.VMEM((nb * LANES, width), jnp.bfloat16),
        pltpu.VMEM((8 * rows, nb * LANES), jnp.float32),
        pltpu.SemaphoreType.DMA((nb,)),
    ]
    if nb == 2:
        outs = (
            jax.ShapeDtypeStruct((8, rows, LANES), jnp.int16),
            pltpu.VMEM((8 * rows, width), jnp.bfloat16),
        )
        scratch.append(pltpu.SemaphoreType.DMA((8,)))
    else:
        outs = jax.ShapeDtypeStruct((8, rows + 64, LANES), jnp.int16)
    return pl.pallas_call(
        functools.partial(products_kernel, nb),
        out_shape=outs,
        in_specs=[pl.BlockSpec(memory_space=pltpu.SMEM), vmem]
        + [anywhere if nb == 2 else vmem] * len(bands)
        + [anywhere] * nb,
        out_specs=(vmem, vmem) if nb == 2 else vmem,
        scratch_shapes=scratch,
        compiler_params=pltpu.CompilerParams(vmem_limit_bytes=24 * 2**20),
        cost_estimate=pl.CostEstimate(
            flops=2 * 8 * rows * nb * LANES * width,
            bytes_accessed=(8 + nb) * rows * width * 2,
            transcendentals=0,
        ),
    )(where, maps, *bands, *rights)


def along_z(z, y, c):
    return z ^ (1 + c), y, c


def per_device(coeffs, shift_maps):
    bands, _, width = coeffs.shape
    position = lax.axis_index("ka")
    core = position & 1
    yy = (position >> 1) & (HALF - 1)
    where = jnp.stack([yy, core]).astype(jnp.int32)
    maps = lax.dynamic_index_in_dim(shift_maps, position >> 3, 0, keepdims=False) & (LANES - 1)
    later_maps = jnp.where(core == 0, maps[1:], jnp.stack([maps[2], maps[1]]))

    def rows_of(shard):
        return shard.transpose(1, 0, 2).reshape(2 * bands, width)

    mine = rows_of(coeffs)
    near = moved(coeffs, to_sibling)
    sibling = rows_of(near)
    za = moved(mine, along_z)
    zb = moved(after(sibling, za), along_z)
    ga, gb, sa, sb = [None], [None], [None], [None]
    for hops in range(1, HALF):
        if hops == 1:
            ga.append(rows_of(moved(coeffs, along_y)))
            gb.append(rows_of(moved(near, along_y)))
        else:
            ga.append(moved(after(ga[-1], za, sa[1], sb[1]) if hops == 3 else ga[-1], along_y))
            gb.append(moved(gb[-1], along_y))
        sa.append(moved(ga[-1], to_sibling, wanted_from_sibling(hops)))
        sb.append(moved(gb[-1], to_sibling, wanted_from_sibling(hops)))
    opposite = moved(after(ga[-1], sa[2], sb[2]), along_y)
    zs = moved(after(zb, ga[-1]), to_sibling)
    lefts = [mine, sibling, *ga[1:], *gb[1:], *sa[1:], *sb[1:]]
    later, packed = products(where, later_maps, lefts, [za, zs])
    every = products(where, maps[:1], [packed, later], [opposite])
    shares = lax.all_to_all(
        every, "ga", 0, 0, axis_index_groups=[[0, 1, 2, 3], [4, 5, 6, 7]], tiled=True
    )
    rows = 2 * bands
    units = jnp.exp2(shares[:, : 3 * bands, rows : rows + 1].astype(jnp.float32))
    sums = shares[:, : 3 * bands, :rows].astype(jnp.float32) * units
    lower, upper = sums[0::2].sum(axis=0), sums[1::2].sum(axis=0)
    low = lax.axis_index("ga") < 4
    theirs = lax.ppermute(jnp.where(low, upper, lower), "ga", [(g, g ^ 4) for g in range(8)])
    total = jnp.where(low, lower, upper) + theirs
    second, third, first = total[:bands], total[bands:rows], total[rows:]
    return jnp.stack([first, second, third], axis=1).reshape(bands, 3, 2, bands)


def solution(mesh):
    return jax.shard_map(
        per_device,
        mesh=mesh,
        in_specs=(P("ka", None, "ga"), P(None, None, "ga")),
        out_specs=P("ga", None, None, "ka"),
        check_vma=False,
    )
```

```python
import functools
import math

import jax
import jax.numpy as jnp
from jax import lax
from jax.experimental import pallas as pl
from jax.experimental.pallas import tpu as pltpu
from jax.sharding import PartitionSpec as P

CORES = 2
YS = 8
HALF = YS // 2
LANES = 128


def place(i):
    return i // (YS * CORES), i // CORES % YS, i % CORES


def number(z, y, c):
    return (z * YS + y % YS) * CORES + c


def moved(shard, target, wanted=None):
    pairs = [(i, number(*target(*place(i)))) for i in range(lax.axis_size("ka"))]
    if wanted is not None:
        pairs = [(s, t) for s, t in pairs if wanted(*place(t))]
    return lax.ppermute(shard, "ka", pairs)


def to_sibling(z, y, c):
    return z, y, 1 - c


def along_y(z, y, c):
    return z, y + 1 - 2 * c, c


def wanted_from_sibling(hops):
    def wanted(z, y, c):
        return hops <= (HALF - 1 - y % HALF if c == 0 else y % HALF)

    return wanted


def after(shard, *others):
    return lax.optimization_barrier((shard, *others))[0]


def scaled(values, exponent_lane):
    most = jnp.max(jnp.abs(values), axis=1, keepdims=True)
    exponent = jnp.maximum(jnp.ceil(jnp.log2(jnp.maximum(most, 1e-36)) - math.log2(32700)), -126.0)
    whole = jnp.round(values * jnp.exp2(-exponent))
    lane = lax.broadcasted_iota(jnp.int32, values.shape, 1)
    return jnp.where(lane == exponent_lane, exponent, whole).astype(jnp.int32).astype(jnp.int16)


def chosen_rows(shift, raw):
    inside = lax.broadcasted_iota(jnp.int32, (LANES, LANES), 0)
    chosen = jnp.where(inside == shift, 1.0, 0.0).astype(jnp.bfloat16)
    return jnp.dot(raw, chosen, preferred_element_type=jnp.float32).astype(jnp.bfloat16)


def signed(sums, half):
    rows = 2 * half
    low = sums[half:]
    spare = jnp.zeros((half, LANES - rows), jnp.float32)
    return sums[:half] + jnp.concatenate([low[:, half:rows], -low[:, :half], spare], axis=1)


def products_kernel(nb, *refs):
    refs = list(refs)
    where, maps = refs[:2]
    del refs[:2]
    yy, core = where[0], where[1]
    reach = jnp.where(core == 0, yy, HALF - 1 - yy)
    if nb == 2:
        own, sibling = refs[:2]
        ga, gb, sa, sb = (refs[2 + 3 * i : 5 + 3 * i] for i in range(4))
        rights = refs[14:16]
        out, left, raw, right, total, raw_sems, left_sems = refs[16:]
    else:
        left, done, *rights = refs[:3]
        out, raw, right, total, raw_sems = refs[3:]
    rows, width = raw.shape[1:]
    half = rows // 2

    def copy(source, s):
        return pltpu.make_async_copy(source, left.at[pl.ds(s * rows, rows)], left_sems.at[s])

    for b in range(nb):
        pltpu.make_async_copy(rights[b], raw.at[b], raw_sems.at[b]).start()
    if nb == 2:
        copy(own, 0).start()
        copy(sibling, 1).start()
        for d in range(1, HALF):
            for part, (near, far) in enumerate(((ga, sb), (gb, sa))):

                @pl.when(d <= reach)
                def _():
                    copy(near[d - 1], 2 * d + part).start()

                @pl.when(d > reach)
                def _():
                    copy(far[HALF - d - 1], 2 * d + part).start()

    spare = jnp.zeros((LANES - rows, width), jnp.bfloat16)
    for b in range(nb):
        right[pl.ds(b * LANES + rows, LANES - rows)] = spare
    for b in range(nb):
        pltpu.make_async_copy(rights[b], raw.at[b], raw_sems.at[b]).wait()
    for i in range(width // LANES):
        at = pl.ds(i * LANES, LANES)
        for b in range(nb):
            right[pl.ds(b * LANES, rows), at] = chosen_rows(maps[b : b + 1, at], raw[b, :, at])
    if nb == 2:
        for s in range(8):
            copy(own, s).wait()
    total[...] = lax.dot_general(
        left[...], right[...], (((1,), (1,)), ((), ())), preferred_element_type=jnp.float32
    )
    if nb == 1:
        out[:, pl.ds(0, rows)] = done[...]
    for s in range(8):
        d, other = s // 2, s % 2
        chip = jnp.where(core == 0, yy + HALF - d, yy + d) & (HALF - 1)
        block = (((chip & 1) << 1) | (core ^ other)) << 1 | (chip >> 1)
        sums = [signed(total[pl.ds(s * rows, rows), pl.ds(b * LANES, LANES)], half) for b in range(nb)]
        if nb == 1:
            spare_rows = jnp.zeros((64 - half, LANES), jnp.float32)
            out[block, pl.ds(rows, 64)] = scaled(jnp.concatenate([sums[0], spare_rows], axis=0), rows)
        else:
            first = jnp.where(core == 0, sums[0], sums[1])
            second = jnp.where(core == 0, sums[1], sums[0])
            out[block] = scaled(jnp.concatenate([first, second], axis=0), rows)


def products(where, maps, bands, rights):
    nb = len(rights)
    rows, width = rights[0].shape
    anywhere = pl.BlockSpec(memory_space=pl.ANY)
    vmem = pl.BlockSpec(memory_space=pltpu.VMEM)
    scratch = [
        pltpu.VMEM((nb, rows, width), jnp.bfloat16),
        pltpu.VMEM((nb * LANES, width), jnp.bfloat16),
        pltpu.VMEM((8 * rows, nb * LANES), jnp.float32),
        pltpu.SemaphoreType.DMA((nb,)),
    ]
    if nb == 2:
        outs = (
            jax.ShapeDtypeStruct((8, rows, LANES), jnp.int16),
            pltpu.VMEM((8 * rows, width), jnp.bfloat16),
        )
        scratch.append(pltpu.SemaphoreType.DMA((8,)))
    else:
        outs = pltpu.VMEM((8, rows + 64, LANES), jnp.int16)
    return pl.pallas_call(
        functools.partial(products_kernel, nb),
        out_shape=outs,
        in_specs=[pl.BlockSpec(memory_space=pltpu.SMEM), vmem]
        + [anywhere if nb == 2 else vmem] * len(bands)
        + [anywhere] * nb,
        out_specs=(vmem, vmem) if nb == 2 else vmem,
        scratch_shapes=scratch,
        compiler_params=pltpu.CompilerParams(vmem_limit_bytes=24 * 2**20),
        cost_estimate=pl.CostEstimate(
            flops=2 * 8 * rows * nb * LANES * width,
            bytes_accessed=(8 + nb) * rows * width * 2,
            transcendentals=0,
        ),
    )(where, maps, *bands, *rights)


def along_z(z, y, c):
    return z ^ (1 + c), y, c


def per_device(coeffs, shift_maps):
    bands, _, width = coeffs.shape
    position = lax.axis_index("ka")
    core = position & 1
    yy = (position >> 1) & (HALF - 1)
    where = jnp.stack([yy, core]).astype(jnp.int32)
    maps = lax.dynamic_index_in_dim(shift_maps, position >> 3, 0, keepdims=False) & (LANES - 1)
    later_maps = jnp.where(core == 0, maps[1:], jnp.stack([maps[2], maps[1]]))
    mine = coeffs.transpose(1, 0, 2).reshape(2 * bands, width)

    sibling = moved(mine, to_sibling)
    za = moved(mine, along_z)
    zb = moved(after(sibling, za), along_z)
    ga, gb, sa, sb = [mine], [sibling], [None], [None]
    for hops in range(1, HALF):
        ga.append(moved(after(ga[-1], za, sa[1], sb[1]) if hops == 3 else ga[-1], along_y))
        gb.append(moved(gb[-1], along_y))
        sa.append(moved(ga[-1], to_sibling, wanted_from_sibling(hops)))
        sb.append(moved(gb[-1], to_sibling, wanted_from_sibling(hops)))
    opposite = moved(after(ga[-1], zb, sa[2], sb[2]), along_y)
    zs = moved(zb, to_sibling)
    lefts = [mine, sibling, *ga[1:], *gb[1:], *sa[1:], *sb[1:]]
    later, packed = products(where, later_maps, lefts, [za, zs])
    every = products(where, maps[:1], [packed, later], [opposite])
    shares = lax.all_to_all(
        every, "ga", 0, 0, axis_index_groups=[[0, 1, 2, 3], [4, 5, 6, 7]], tiled=True
    )
    rows = 2 * bands
    units = jnp.exp2(shares[:, : 3 * bands, rows : rows + 1].astype(jnp.float32))
    sums = shares[:, : 3 * bands, :rows].astype(jnp.float32) * units
    lower, upper = sums[0::2].sum(axis=0), sums[1::2].sum(axis=0)
    low = lax.axis_index("ga") < 4
    theirs = lax.ppermute(jnp.where(low, upper, lower), "ga", [(g, g ^ 4) for g in range(8)])
    total = jnp.where(low, lower, upper) + theirs
    second, third, first = total[:bands], total[bands:rows], total[rows:]
    return jnp.stack([first, second, third], axis=1).reshape(bands, 3, 2, bands)


def solution(mesh):
    return jax.shard_map(
        per_device,
        mesh=mesh,
        in_specs=(P("ka", None, "ga"), P(None, None, "ga")),
        out_specs=P("ga", None, None, "ka"),
        check_vma=False,
    )
```
